256 devices in a mesh: row: 8 (over y_hi, x), col: 32 (over z, y_lo, core).
Axes of the slice: x: 4, y: 4 (y_hi: 2, y_lo: 2; y = y_hi * 2 + y_lo), z: 8, core: 2. Of those that a mesh axis runs over, the one named last changes fastest.
Arguments:
- inputs: bfloat16 [1024, 12288], P('col', 'row'), may hold values from -6 to 6
- grad_out: bfloat16 [1024, 12288], P('col', 'row'), may hold values from -6 to 6
- pre_act: bfloat16 [1024, 24576], P('row', 'col'), may hold values from -6 to 6
- w_in: bfloat16 [12288, 24576], P('row', 'col'), may hold values from -0.0390625 to 0.0390625
- w_out: bfloat16 [24576, 12288], P('col', 'row'), may hold values from -0.0546875 to 0.0546875
- mask_in: int32 [96, 192], P('row', 'col'), may hold values from 0 to 1, as said below
- mask_out: int32 [192, 96], P('col', 'row'), may hold values from 0 to 1, as said below
Outputs:
- grad_inputs: bfloat16 [1024, 12288], P('col', 'row')
- grad_w_in: bfloat16 [12288, 24576], P('row', 'col')
- grad_w_out: bfloat16 [24576, 12288], P('col', 'row')
The draws below stay inside these ranges and needn't reach their ends.
Inputs may be any that keep to these rules, and one draw needn't show every extreme that they name: `mask_in`: each entry is 0 or 1; the share of ones differs from one row of tiles to another. `mask_out`: each entry is 0 or 1; the share of ones differs from one row of tiles to another.
All inputs are finite; a program needn't handle non-finite values.
Results may differ from the reference program's by a relative error of at most 0.0049.
Values may be sent and summed in bfloat16 or wider, within the bound.
No kernel may reach another device: no remote copies, remote signals or barrier semaphores. Data moves between devices by JAX's collectives and lax.ppermute only.
A program may use at most 128 MiB of HBM per device.

```python
import math
import jax
import jax.numpy as jnp

D = 12288
FF = 24576
TILE = 128
TOKENS = 1024
DT = 96
FT = 192


def tile_mask(key, rows, cols):
    first, second = jax.random.split(key)
    density = jax.random.randint(first, (rows, 1), 1, 8)
    draws = jax.random.randint(second, (rows, cols), 0, 16)
    return (draws < density).astype(jnp.int32)


def draw_mask_in(key, part):
    key = jax.random.fold_in(key, 11)
    return tile_mask(key, DT, FT)


def draw_mask_out(key, part):
    key = jax.random.fold_in(key, 23)
    return tile_mask(key, FT, DT)


def block_levels(key, extent, pieces, least, top_value):
    def one(dim, shards_of):
        heights = jax.random.uniform(jax.random.fold_in(jax.random.fold_in(key, 6), dim), (shards_of,), jnp.float32, least / len(pieces), top_value / len(pieces))
        return jnp.repeat(jnp.exp(heights), extent[dim] // shards_of).reshape((-1,) + (1,) * (len(extent) - dim - 1))

    gain = one(*pieces[0])
    for cut in pieces[1:]:
        gain = gain * one(*cut)
    return gain


def noise(key, dims, scale, reach, pieces=(), held_as=jnp.bfloat16):
    values = scale * jax.random.normal(key, dims, jnp.float32)
    if pieces:
        values = values * block_levels(key, dims, pieces, -0.22, 0.18)
    return jnp.clip(values, -reach, reach).astype(held_as)


def setup_inputs(seed: int = 0) -> dict:
    seeds = jax.random.split(jax.random.key(seed), 8)
    return {
        "inputs": noise(seeds[0], (TOKENS, D), 1.0, 6.0, ((0, 32), (1, 8))),
        "grad_out": noise(seeds[1], (TOKENS, D), 1.0, 6.0, ((0, 32), (1, 8))),
        "pre_act": noise(seeds[2], (TOKENS, FF), 1.5, 6.0, ((0, 8), (1, 32))),
        "w_in": noise(seeds[3], (D, FF), FF ** -0.5, 0.0390625, ((0, 8), (1, 32))),
        "w_out": noise(seeds[4], (FF, D), D ** -0.5, 0.0546875, ((0, 32), (1, 8))),
        "mask_in": draw_mask_in(jax.random.fold_in(seeds[7], 71), 0),
        "mask_out": draw_mask_out(jax.random.fold_in(seeds[7], 71), 0),
    }


coef = math.sqrt(2.0 / math.pi)

def spread(mask):
    return jnp.repeat(jnp.repeat(mask, TILE, 0), TILE, 1).astype(jnp.bfloat16)

def reference(inputs, grad_out, pre_act, w_in, w_out, mask_in, mask_out):
    masked_in = w_in * spread(mask_in)
    masked_out = w_out * spread(mask_out)
    hidden_grad = jnp.dot(grad_out, masked_out.T, preferred_element_type=jnp.float32)
    zval = pre_act.astype(jnp.float32)
    tval = jnp.tanh(coef * (zval + 0.044715 * zval ** 3))
    deriv = 0.5 * (1.0 + tval) + 0.5 * zval * (1.0 - tval * tval) * coef * (1.0 + 3.0 * 0.044715 * zval * zval)
    act_grad = (hidden_grad * deriv).astype(jnp.bfloat16)
    hidden = (0.5 * zval * (1.0 + tval)).astype(jnp.bfloat16)
    grad_inputs = jnp.dot(act_grad, masked_in.T, preferred_element_type=jnp.float32).astype(jnp.bfloat16)
    grad_w_in = (jnp.dot(inputs.T, act_grad, preferred_element_type=jnp.float32) * spread(mask_in)).astype(jnp.bfloat16)
    grad_w_out = (jnp.dot(hidden.T, grad_out, preferred_element_type=jnp.float32) * spread(mask_out)).astype(jnp.bfloat16)
    return (grad_inputs, grad_w_in, grad_w_out)
```

```python
import functools
import math

import jax
import jax.numpy as jnp
from jax import lax
from jax.experimental import pallas as pl
from jax.experimental.pallas import tpu as pltpu
from jax.sharding import Mesh
from jax.sharding import PartitionSpec as P

coef = math.sqrt(2.0 / math.pi)
VMEM = 20
BF = jnp.bfloat16
F32 = jnp.float32
SIZE = {"yhi": 2, "x": 4, "z": 8, "ylo": 2, "core": 2}
NT = (((1,), (1,)), ((), ()))
TN = (((0,), (0,)), ((), ()))
MIB = 1 << 20


def shift(value, axis, by):
    count = SIZE[axis]
    return lax.ppermute(value, axis, [(i, (i + by) % count) for i in range(count)])


def params(mib):
    return pltpu.CompilerParams(vmem_limit_bytes=mib * MIB)


def cost(flops, size):
    return pl.CostEstimate(flops=flops, bytes_accessed=size, transcendentals=0)


def after(value, *others):
    return lax.optimization_barrier((value, *others))[0]


def gather_z(rows):
    count = rows.shape[0]
    other = shift(rows, "ylo", 1)
    own = jnp.concatenate([rows, other])
    pieces = [(own, [(0, 0, 0), (count, 0, 1)])]
    up = down = own
    for step in range(1, 4):
        up, down = shift(up, "z", 1), shift(down, "z", -1)
        pieces.append((up, [(0, -step, 0), (count, -step, 1)]))
        pieces.append((down, [(0, step, 0), (count, step, 1)]))
    up, down = shift(up[:count], "z", 1), shift(down[count:], "z", -1)
    pieces.append((up, [(0, 4, 0)]))
    pieces.append((down, [(0, 4, 1)]))
    return pieces


def gather_x(rows, beside=None):
    count = rows.shape[0]
    other = shift(rows, "yhi", 1)
    own = jnp.concatenate([rows, other])
    up, down = shift(own, "x", 1), shift(own, "x", -1)
    far = (up[:count], down[count:])
    if beside is not None:
        far = lax.optimization_barrier((*far, beside(own)))[:2]
    far_up, far_down = shift(far[0], "x", 1), shift(far[1], "x", -1)
    both = lambda off: [(0, off, 0), (count, off, 1)]
    return [
        (own, both(0)),
        (up, both(-1)),
        (down, both(1)),
        (far_up, [(0, 2, 0)]),
        (far_down, [(0, 2, 1)]),
    ]


def whole(shape):
    return pl.BlockSpec(shape, lambda *_: (0,) * len(shape))


def place_z(pos, off, half, count):
    owner = lax.rem(pos[2] + (off + 8), 8)
    return pl.multiple_of(owner * (2 * count) + lax.rem(pos[3] + half, 2) * count, 16)


def place_x(pos, off, half, count):
    owner = lax.rem(pos[0] + half, 2) * 4 + lax.rem(pos[1] + (off + 4), 4)
    return pl.multiple_of(owner * count, 16)


def in_vmem(count):
    return [pl.BlockSpec(memory_space=pltpu.VMEM)] * count


def call(kernel, name, pos, arrays, shapes, scratch, flops):
    return pl.pallas_call(
        kernel,
        in_specs=[pl.BlockSpec(memory_space=pltpu.SMEM)] + in_vmem(len(arrays)),
        out_specs=in_vmem(len(shapes)),
        out_shape=[jax.ShapeDtypeStruct(n, t) for n, t in shapes],
        scratch_shapes=scratch,
        compiler_params=params(VMEM),
        cost_estimate=cost(flops, MIB),
        name=name,
    )(pos, *arrays)


def assemble(plan, pieces, place, size, pos, out):
    for ref, spots in zip(pieces, plan):
        for first, off, half in spots:
            out[pl.ds(place(pos, off, half), size), :] = ref[first : first + size, :]


def first_kernel(plan, count, pos, *refs):
    pieces = refs[: len(plan)]
    own_ref, peer_ref, rows, up1, up2, down1, down2, keep, held = refs[len(plan) :]
    two = 2 * count
    wide = held.shape[1]
    at = lambda p, off, half: place_z(p, off, half, count)
    assemble(plan, pieces, at, count, pos, rows)

    for half, weight in enumerate((own_ref, peer_ref)):

        @pl.loop(0, 768 // wide)
        def _(step):
            first = pl.multiple_of(step * wide, wide)
            held[...] = lax.dot_general(
                rows[...], weight[pl.ds(first, wide), :], NT, preferred_element_type=F32
            )
            where = pl.ds(pl.multiple_of(half * 768 + first, 128), wide)

            def block(off, y):
                return held[pl.ds(place_x(pos, off, y, two), two), :]

            up1[0:two, where] = block(2, 0).astype(BF)
            up1[two : 2 * two, where] = block(1, 1).astype(BF)
            up2[:, where] = block(1, 0)
            down1[0:two, where] = block(2, 1).astype(BF)
            down1[two : 2 * two, where] = block(-1, 0).astype(BF)
            down2[:, where] = block(-1, 1)
            keep[0:two, where] = block(0, 0)
            keep[two : 2 * two, where] = block(0, 1)


def first(pos, pieces, own, peer, count):
    tokens, two = 16 * count, 2 * count
    heights = [(tokens, BF), (2 * two, BF), (two, F32), (2 * two, BF), (two, F32), (2 * two, F32)]
    return call(
        functools.partial(first_kernel, [s for _, s in pieces], count),
        "first",
        pos,
        [a for a, _ in pieces] + [own, peer],
        [((n, 1536), t) for n, t in heights],
        [pltpu.VMEM((tokens, 384), F32)],
        4 * tokens * 1536 * 1536,
    )


def second_kernel(plan, count, pos, *refs):
    pieces = refs[: len(plan)]
    own_ref, peer_ref, rows, rows_peer = refs[len(plan) : len(plan) + 4]
    outs = refs[len(plan) + 4 : -1]
    held = refs[-1]
    two = 2 * count
    wide = held.shape[1]
    for ref, spots in zip(pieces, plan):
        for first, off, half in spots:
            at = pl.ds(place_x(pos, off, half, two), two)
            rows[at, :] = ref[first : first + two, 0:768]
            rows_peer[at, :] = ref[first : first + two, 768:1536]

    @pl.loop(0, 1536 // wide)
    def _(step):
        where = pl.ds(pl.multiple_of(step * wide, wide), wide)
        out = lax.dot_general(rows[...], own_ref[where, :], NT, preferred_element_type=F32)
        out += lax.dot_general(rows_peer[...], peer_ref[where, :], NT, preferred_element_type=F32)
        held[...] = out

        def block(off, half):
            return held[pl.ds(place_z(pos, off, half, count), count), :]

        up, down, keep = outs[0:4], outs[4:8], outs[8]
        for s in range(4):
            kind = BF if s == 0 else F32
            up[s][0:count, where] = block(4 - s, 0).astype(kind)
            down[s][0:count, where] = block(s - 4, 1).astype(kind)
            if s < 3:
                up[s][count:two, where] = block(3 - s, 1).astype(kind)
                down[s][count:two, where] = block(s - 3, 0).astype(kind)
        keep[0:count, where] = block(0, 0)
        keep[count:two, where] = block(0, 1)


def second(pos, pieces, own, peer, count):
    tokens, two = 16 * count, 2 * count
    ring = [(two, BF), (two, F32), (two, F32), (count, F32)]
    shapes = [((tokens, 768), BF)] * 2
    shapes += [((n, 1536), t) for n, t in ring + ring + [(two, F32)]]
    return call(
        functools.partial(second_kernel, [s for _, s in pieces], count),
        "second",
        pos,
        [a for a, _ in pieces] + [own, peer],
        shapes,
        [pltpu.VMEM((tokens, 512), F32)],
        4 * tokens * 1536 * 1536,
    )


def collect_kernel(plan, count, pos, *refs):
    at = lambda p, off, half: place_z(p, off, half, count)
    assemble(plan, refs[:-1], at, count, pos, refs[-1])


def collect(pos, pieces, count):
    kernel = functools.partial(collect_kernel, [s for _, s in pieces], count)
    arrays = [a for a, _ in pieces]
    return call(kernel, "collect", pos, arrays, [((16 * count, 1536), BF)], [], 0)[0]


def store_kept(total, mask, first, out):
    for tile in range(out.shape[0] // 128):
        rows = slice(tile * 128, tile * 128 + 128)
        out[rows, :] = (total[rows, :] * mask[pl.ds(first + tile, 1), :]).astype(BF)


def wout_kernel(plan, pos, *refs):
    pieces = refs[: len(plan)]
    own, peer, mask, out, held = refs[len(plan) :]
    for ref, spots in zip(pieces, plan):
        for first, off, half in spots:
            owner = lax.rem(pos[0] + half, 2) * 4 + lax.rem(pos[1] + (off + 4), 4)
            held[owner] = ref[first : first + 128, :].reshape(2, 2, 32, -1)
    total = None
    for k, part in enumerate((own, peer)):
        left = held[:, :, lax.rem(pos[4] + k, 2)].reshape(512, -1)
        term = lax.dot_general(left, part[...], TN, preferred_element_type=F32)
        total = term if total is None else total + term
    store_kept(total, mask, pl.program_id(0) * (out.shape[0] // 128), out)


def wout_grad(pos, pieces, own, peer, mask):
    arrays = [a for a, _ in pieces]
    block = 384
    return pl.pallas_call(
        functools.partial(wout_kernel, [s for _, s in pieces]),
        grid_spec=pltpu.PrefetchScalarGridSpec(
            num_scalar_prefetch=1,
            grid=(768 // block,),
            in_specs=[pl.BlockSpec((a.shape[0], block), lambda i, _: (0, i)) for a in arrays]
            + in_vmem(3),
            out_specs=pl.BlockSpec((block, 1536), lambda i, _: (i, 0)),
            scratch_shapes=[pltpu.VMEM((8, 2, 2, 32, block), BF)],
        ),
        out_shape=jax.ShapeDtypeStruct((768, 1536), BF),
        compiler_params=params(VMEM),
        cost_estimate=cost(4 * 1024 * 1536 * 768, 8 * MIB),
        name="wout_grad",
    )(pos, *arrays, own, peer, mask)


def win_kernel(left0, left1, own, peer, mask, out):
    total = None
    for left, right in ((left0, own), (left1, peer)):
        term = lax.dot_general(left[...], right[...], TN, preferred_element_type=F32)
        total = term if total is None else total + term
    store_kept(total, mask, pl.program_id(0) * (out.shape[0] // 128), out)


def win_grad(ins, ins_peer, own, peer, mask):
    block = 768
    rows = pl.BlockSpec((512, block), lambda i: (0, i))
    return pl.pallas_call(
        win_kernel,
        grid=(1536 // block,),
        in_specs=[rows, rows] + in_vmem(3),
        out_specs=pl.BlockSpec((block, 768), lambda i: (i, 0)),
        out_shape=jax.ShapeDtypeStruct((1536, 768), BF),
        compiler_params=params(VMEM),
        cost_estimate=cost(4 * 1024 * 1536 * 768, 8 * MIB),
        name="win_grad",
    )(ins, ins_peer, own, peer, mask)


def slope(values):
    zval = values.astype(F32)
    tval = jnp.tanh(coef * (zval + 0.044715 * zval**3))
    return 0.5 * (1.0 + tval) + 0.5 * zval * (1.0 - tval * tval) * coef * (
        1.0 + 3.0 * 0.044715 * zval * zval
    )


def body(inputs, grad_out, pre_act, w_in, w_out, mask_in, mask_out):
    axis = lax.axis_index
    names = ("yhi", "x", "z", "ylo", "core")
    pos = jnp.stack([axis(n) for n in names]).astype(jnp.int32)
    core = axis("core")
    side = 128
    f = lambda v: v.astype(F32)

    def masked(weight, mask):
        rows, cols = mask.shape
        keep = jnp.broadcast_to(mask[:, None, :, None], (rows, side, cols, side))
        return weight * keep.reshape(rows * side, cols * side).astype(BF)

    count, two = 32, 64
    grad_pieces = gather_z(grad_out)

    zval = f(pre_act)
    tval = jnp.tanh(coef * (zval + 0.044715 * zval**3))
    hidden = (0.5 * zval * (1.0 + tval)).astype(BF)
    hidden_pieces = gather_x(hidden)

    out_own = masked(after(w_out, grad_pieces[0][0]), mask_out)
    out_peer = shift(out_own, "core", 1)
    in_own = masked(after(w_in, out_own), mask_in)
    in_peer = shift(in_own, "core", 1)

    pre = pre_act.reshape(2, 2, 32, 768)
    split = lambda k: lax.dynamic_index_in_dim(pre, k, 1, False).reshape(64, 768)
    pre_own = split(core)
    pre_peer = shift(after(split(1 - core), out_own), "core", 1)
    slopes = jnp.concatenate([slope(pre_own), slope(pre_peer)], axis=1)
    spread_in = jnp.repeat(f(mask_in), side, axis=1)
    spread_out = jnp.repeat(f(mask_out), side, axis=1)

    ready = after(pos, hidden_pieces[-1][0], hidden_pieces[-2][0], in_own, slopes, spread_in, spread_out)
    rows, up1, up2, down1, down2, keep = first(ready, grad_pieces, out_own, out_peer, count)
    input_pieces = gather_z(after(inputs, grad_pieces[-1][0], grad_pieces[-2][0]))
    up1, down1 = shift(up1, "x", 1), shift(down1, "x", -1)
    rows_peer = shift(rows, "core", 1)
    up2 = (up2 + f(up1[:two])).astype(BF)
    down2 = (down2 + f(down1[:two])).astype(BF)
    up2, down2 = shift(up2, "x", 1), shift(down2, "x", -1)
    send = (keep[two:] + f(up1[two:]) + f(down2)).astype(BF)
    mine = keep[:two] + f(down1[two:]) + f(up2)
    total = mine + f(shift(send, "yhi", 1))
    act = (total * slopes).astype(BF)
    made = []

    def beside(own):
        made.append(wout_grad(pos, hidden_pieces, rows, after(rows_peer, own), spread_out))
        return made[0]

    act_pieces = gather_x(act, beside)
    ins = collect(pos, input_pieces, count)
    ins_peer = shift(ins, "core", 1)
    ready = after(pos, ins)
    outs = second(ready, act_pieces, in_own, in_peer, count)
    acts_own, acts_peer = outs[0:2]
    up, down, keep = outs[2:6], outs[6:10], outs[10]
    send_up, send_down = up[0], down[0]
    for s in range(1, 4):
        got_up, got_down = shift(send_up, "z", 1), shift(send_down, "z", -1)
        if s == 1:
            acts_peer = shift(acts_peer, "core", 1)
        elif s == 2:
            grad_w_in = win_grad(
                ins, ins_peer, acts_own, after(acts_peer, send_up, send_down), spread_in
            )
            got_up, got_down, _ = lax.optimization_barrier((got_up, got_down, grad_w_in))
        n = two if s < 3 else count
        send_up = (up[s] + f(got_up[:n])).astype(BF)
        send_down = (down[s] + f(got_down[:n])).astype(BF)
    end_up, end_down = shift(send_up, "z", 1), shift(send_down, "z", -1)
    send = (keep[count:] + f(got_up[count:]) + f(end_down)).astype(BF)
    mine = keep[:count] + f(got_down[count:]) + f(end_up)
    grad_inputs = (mine + f(shift(send, "ylo", 1))).astype(BF)
    return grad_inputs, grad_w_in, made[0]


def solution(mesh):
    fine = Mesh(mesh.devices.reshape(2, 4, 8, 2, 2), ("yhi", "x", "z", "ylo", "core"))
    row, col = ("yhi", "x"), ("z", "ylo", "core")
    return jax.shard_map(
        body,
        mesh=fine,
        in_specs=(
            P(col, row),
            P(col, row),
            P(row, col),
            P(row, col),
            P(col, row),
            P(row, col),
            P(col, row),
        ),
        out_specs=(P(col, row), P(row, col), P(col, row)),
        check_vma=False,
    )
```

```python
import functools
import math

import jax
import jax.numpy as jnp
from jax import lax
from jax.experimental import pallas as pl
from jax.experimental.pallas import tpu as pltpu
from jax.sharding import Mesh
from jax.sharding import PartitionSpec as P

coef = math.sqrt(2.0 / math.pi)
VMEM = 16
BF = jnp.bfloat16
F32 = jnp.float32
SIZE = {"yhi": 2, "x": 4, "z": 8, "ylo": 2, "core": 2}
TO_X = (
    (2, 1, BF),
    (-1, 1, BF),
    (1, 1, F32),
    (2, 0, BF),
    (1, 0, BF),
    (-1, 0, F32),
    (0, 0, F32),
    (0, 1, F32),
)
FROM_X = ((0, 0), (0, 1), (-1, 0), (1, 0), (-1, 1), (1, 1), (2, 0), (2, 1))
NT = (((1,), (1,)), ((), ()))
TN = (((0,), (0,)), ((), ()))
MIB = 1 << 20


def shift(value, axis, by):
    count = SIZE[axis]
    return lax.ppermute(value, axis, [(i, (i + by) % count) for i in range(count)])


def params(mib):
    return pltpu.CompilerParams(vmem_limit_bytes=mib * MIB)


def cost(flops, size):
    return pl.CostEstimate(flops=flops, bytes_accessed=size, transcendentals=0)


def after(value, *others):
    return lax.optimization_barrier((value, *others))[0]


def together(*values):
    return lax.optimization_barrier(values)


def both_ways(axis, up, down):
    return shift(up, axis, 1), shift(down, axis, -1)


def plan_z(count):
    half = lambda off, kind, at: [(at, off, 0, kind), (at + count, off, 1, kind)]
    both = lambda off: half(off, 0, 0) + half(off, 1, 2 * count)
    plan = [both(0)]
    for step in range(1, 4):
        plan += [both(-step), both(step)]
    return plan + [half(4, 0, 0), half(4, 1, 0)]


def plan_x(count):
    both = lambda off: [(0, off, 0), (count, off, 1)]
    return [both(0), both(-1), both(1), both(2)]


def whole(shape):
    return pl.BlockSpec(shape, lambda *_: (0,) * len(shape))


def place_z(pos, off, half, count):
    owner = lax.rem(pos[2] + (off + 8), 8)
    return pl.multiple_of(owner * (2 * count) + lax.rem(pos[3] + half, 2) * count, 16)


def place_x(pos, off, half, count):
    owner = lax.rem(pos[0] + half, 2) * 4 + lax.rem(pos[1] + (off + 4), 4)
    return pl.multiple_of(owner * count, 16)


def in_vmem(count):
    return [pl.BlockSpec(memory_space=pltpu.VMEM)] * count


def call(kernel, name, pos, arrays, shapes, scratch, flops):
    return pl.pallas_call(
        kernel,
        in_specs=[pl.BlockSpec(memory_space=pltpu.SMEM)] + in_vmem(len(arrays)),
        out_specs=in_vmem(len(shapes)),
        out_shape=[jax.ShapeDtypeStruct(n, t) for n, t in shapes],
        scratch_shapes=scratch,
        compiler_params=params(VMEM),
        cost_estimate=cost(flops, MIB),
        name=name,
    )(pos, *arrays)


def kept(mask, row, col, values):
    return jnp.where(mask[row, col] > 0, values, jnp.zeros_like(values))


def mask_kernel(mask_out, mask_in, w_out, w_in, theirs, out):
    out[1536:1600, 0:768] = theirs[...]
    out[1536:1600, 768:1536] = theirs[...]

    @pl.loop(0, 6)
    def _(i):
        rows = pl.ds(pl.multiple_of(i * 128, 128), 128)
        later = pl.ds(pl.multiple_of(i * 128 + 768, 128), 128)
        for j in range(12):
            cols = slice(j * 128, j * 128 + 128)
            out[rows, cols] = kept(mask_out, i, j, w_out[rows, cols])
            side, tile = j // 6, j % 6
            source = pl.ds(pl.multiple_of(i * 128 + side * 768, 128), 128)
            part = w_in[source, tile * 128 : tile * 128 + 128]
            out[later, cols] = kept(mask_in, i + side * 6, tile, part)


def masked(mask_out, mask_in, w_out, w_in, theirs):
    return pl.pallas_call(
        mask_kernel,
        in_specs=[pl.BlockSpec(memory_space=pltpu.SMEM)] * 2 + in_vmem(3),
        out_specs=pl.BlockSpec(memory_space=pltpu.VMEM),
        out_shape=jax.ShapeDtypeStruct((1600, 1536), BF),
        compiler_params=params(VMEM),
        cost_estimate=cost(0, 4 * MIB),
        name="masked",
    )(mask_out, mask_in, w_out, w_in, theirs)


def values_kernel(pos, pre, hidden, slopes, other):
    core = pos[4]
    zval = pre[...].astype(F32)
    tval = jnp.tanh(coef * (zval + 0.044715 * zval**3))
    hidden[...] = (0.5 * zval * (1.0 + tval)).astype(BF)
    for half in range(2):
        mine = pl.ds(pl.multiple_of(half * 64 + core * 32, 32), 32)
        theirs = pl.ds(pl.multiple_of(half * 64 + (1 - core) * 32, 32), 32)
        rows = slice(half * 32, half * 32 + 32)
        slopes[rows, :] = slope(pre[mine, :])
        other[rows, :] = pre[theirs, :]


def first_kernel(plan, count, pos, *refs):
    pieces = refs[: len(plan)]
    own_ref, peer_ref, rows = refs[len(plan) : len(plan) + 3]
    outs, held = refs[len(plan) + 3 : -1], refs[-1]
    two = 2 * count
    for ref, spots in zip(pieces, plan):
        for first, off, half, kind in spots:
            at = pl.ds(place_z(pos, off, half, count) + kind * 16 * count, count)
            rows[at, :] = ref[first : first + count, :]

    for half, weight in enumerate((own_ref, peer_ref)):
        held[...] = lax.dot_general(
            rows[0 : 16 * count, :], weight[0:768, :], NT, preferred_element_type=F32
        )
        where = slice(half * 768, half * 768 + 768)

        for ref, (off, y, _) in zip(outs, TO_X):
            block = held[pl.ds(place_x(pos, off, y, two), two), :]
            ref[:, where] = block.astype(ref.dtype)


def first(pos, pieces, own, peer, count):
    tokens, two = 16 * count, 2 * count
    heights = [(2 * tokens, BF)] + [(two, kind) for _, _, kind in TO_X]
    return call(
        functools.partial(first_kernel, plan_z(count), count),
        "first",
        pos,
        [*pieces, own, peer],
        [((n, 1536), t) for n, t in heights],
        [pltpu.VMEM((tokens, 768), F32)],
        4 * tokens * 1536 * 1536,
    )


def second_kernel(count, pos, *refs):
    pieces, refs = refs[: len(FROM_X)], refs[len(FROM_X) :]
    own_ref, peer_ref, rows, rows_peer = refs[:4]
    outs = refs[4:-1]
    held = refs[-1]
    two = 2 * count
    wide = held.shape[1]
    for ref, (off, y) in zip(pieces, FROM_X):
        at = pl.ds(place_x(pos, off, y, two), two)
        rows[at, :] = ref[:, 0:768]
        rows_peer[at, :] = ref[:, 768:1536]

    for step in range(1536 // wide):
        where = slice(step * wide, step * wide + wide)
        out = lax.dot_general(rows[...], own_ref[768:1536, where], NT, preferred_element_type=F32)
        out += lax.dot_general(rows_peer[...], peer_ref[768:1536, where], NT, preferred_element_type=F32)
        held[...] = out

        def block(off, half):
            return held[pl.ds(place_z(pos, off, half, count), count), :]

        up, down, keep = outs[0:4], outs[4:8], outs[8]
        for s in range(4):
            kind = BF if s == 0 else F32
            up[s][0:count, where] = block(4 - s, 0).astype(kind)
            down[s][0:count, where] = block(s - 4, 1).astype(kind)
            if s < 3:
                up[s][count:two, where] = block(3 - s, 1).astype(kind)
                down[s][count:two, where] = block(s - 3, 0).astype(kind)
        keep[0:count, where] = block(0, 0)
        keep[count:two, where] = block(0, 1)


def second(pos, pieces, own, peer, count):
    tokens, two = 16 * count, 2 * count
    ring = [(two, BF), (two, F32), (two, F32), (count, F32)]
    shapes = [((tokens, 768), BF)] * 2
    shapes += [((n, 1536), t) for n, t in ring + ring + [(two, F32)]]
    return call(
        functools.partial(second_kernel, count),
        "second",
        pos,
        [*pieces, own, peer],
        shapes,
        [pltpu.VMEM((tokens, 768), F32)],
        4 * tokens * 1536 * 1536,
    )


def store_kept(total, mask, first, out):
    for i in range(out.shape[0] // 128):
        rows = slice(i * 128, i * 128 + 128)
        for j in range(out.shape[1] // 128):
            cols = slice(j * 128, j * 128 + 128)
            out[rows, cols] = kept(mask, first + i, j, total[rows, cols]).astype(BF)


def wout_kernel(plan, pos, mask, *refs):
    pieces = refs[: len(plan)]
    own, peer, out, held = refs[len(plan) :]
    for ref, spots in zip(pieces, plan):
        for first, off, half in spots:
            owner = lax.rem(pos[0] + half, 2) * 4 + lax.rem(pos[1] + (off + 4), 4)
            held[owner] = ref[first : first + 128, :].reshape(2, 2, 32, -1)
    total = None
    for k, part in enumerate((own, peer)):
        left = held[:, :, lax.rem(pos[4] + k, 2)].reshape(512, -1)
        term = lax.dot_general(left, part[0:512, :], TN, preferred_element_type=F32)
        total = term if total is None else total + term
    store_kept(total, mask, pl.program_id(0) * (out.shape[0] // 128), out)


def wout_grad(pos, pieces, own, peer, mask):
    block = 384
    return pl.pallas_call(
        functools.partial(wout_kernel, plan_x(128)),
        grid_spec=pltpu.PrefetchScalarGridSpec(
            num_scalar_prefetch=2,
            grid=(768 // block,),
            in_specs=[pl.BlockSpec((a.shape[0], block), lambda i, *_: (0, i)) for a in pieces]
            + in_vmem(2),
            out_specs=pl.BlockSpec((block, 1536), lambda i, *_: (i, 0)),
            scratch_shapes=[pltpu.VMEM((8, 2, 2, 32, block), BF)],
        ),
        out_shape=jax.ShapeDtypeStruct((768, 1536), BF),
        compiler_params=params(VMEM),
        cost_estimate=cost(4 * 1024 * 1536 * 768, 8 * MIB),
        name="wout_grad",
    )(pos, mask, *pieces, own, peer)


def win_kernel(mask, left0, left1, own, peer, out):
    total = None
    for left, right in ((left0, own), (left1, peer)):
        term = lax.dot_general(left[...], right[...], TN, preferred_element_type=F32)
        total = term if total is None else total + term
    store_kept(total, mask, pl.program_id(0) * (out.shape[0] // 128), out)


def win_grad(own_rows, peer_rows, own, peer, mask):
    block = 768
    rows = pl.BlockSpec((512, block), lambda i, _: (1, i))
    return pl.pallas_call(
        win_kernel,
        grid_spec=pltpu.PrefetchScalarGridSpec(
            num_scalar_prefetch=1,
            grid=(1536 // block,),
            in_specs=[rows, rows] + in_vmem(2),
            out_specs=pl.BlockSpec((block, 768), lambda i, _: (i, 0)),
        ),
        out_shape=jax.ShapeDtypeStruct((1536, 768), BF),
        compiler_params=params(VMEM),
        cost_estimate=cost(4 * 1024 * 1536 * 768, 8 * MIB),
        name="win_grad",
    )(mask, own_rows, peer_rows, own, peer)


def slope(values):
    zval = values.astype(F32)
    tval = jnp.tanh(coef * (zval + 0.044715 * zval**3))
    return 0.5 * (1.0 + tval) + 0.5 * zval * (1.0 - tval * tval) * coef * (
        1.0 + 3.0 * 0.044715 * zval * zval
    )


def body(inputs, grad_out, pre_act, w_in, w_out, mask_in, mask_out):
    names = ("yhi", "x", "z", "ylo", "core")
    pos = jnp.stack([lax.axis_index(n) for n in names]).astype(jnp.int32)
    f = lambda v: v.astype(F32)
    count, two = 32, 64

    others = [shift(v, "ylo", 1) for v in (grad_out, inputs)]
    shapes = [((128, 768), BF), ((64, 768), F32), ((64, 768), BF)]
    hidden, slopes, theirs = call(values_kernel, "values", pos, [pre_act], shapes, [], MIB)
    hidden_other = shift(hidden, "yhi", 1)
    *others, hidden, theirs = together(*others, hidden, theirs)
    sent = jnp.concatenate([grad_out, others[0], inputs, others[1]])
    up1, down1 = both_ways("z", sent, sent)
    own = masked(after(mask_out, sent), mask_in, w_out, w_in, theirs)
    up1, down1, own, hidden_other = together(up1, down1, own, hidden_other)
    up2, down2 = both_ways("z", up1, down1)
    peer = shift(own, "core", 1)
    hid = jnp.concatenate([hidden, hidden_other])
    hid_up, hid_down = both_ways("x", hid, hid)
    up2, down2 = together(up2, down2)
    up3, down3 = both_ways("z", up2, down2)
    up3, down3, hid_up, hid_down = together(up3, down3, hid_up, hid_down)
    up4, down4 = both_ways("z", up3[: 2 * count], down3[2 * count :])
    hid_far = shift(after(hid_up, up3), "x", 1)
    up4, down4, hid_far = together(up4, down4, hid_far)
    pieces = [sent, up1, down1, up2, down2, up3, down3, up4, down4]

    rows, far1, down1, up1, far0, up0, down0, keep0, keep1 = first(pos, pieces, own, peer, count)
    got, down1 = both_ways("x", far1, down1)
    slopes = jnp.concatenate([slopes, slope(after(peer, keep1)[1536:, :768])], axis=1)
    rows_peer = shift(after(rows, slopes), "core", 1)
    got, down1, slopes = together(got, down1, slopes)
    up1, got = both_ways("x", (up1 + f(got)).astype(BF), far0)
    up1, got = together(up1, got)
    other = shift((keep1 + f(down1) + f(up1)).astype(BF), "yhi", 1)
    up0, down0 = both_ways("x", up0, (down0 + f(got)).astype(BF))
    act = ((keep0 + f(up0) + f(down0) + f(other)) * slopes).astype(BF)

    other = shift(act, "yhi", 1)
    up0, down0 = both_ways("x", act, act)
    hidden_pieces = [hid, hid_up, hid_down, hid_far]
    grad_w_out = wout_grad(pos, hidden_pieces, rows, after(rows_peer, act), mask_out)
    other, up0, down0, grad_w_out = together(other, up0, down0, grad_w_out)
    up1, down1 = both_ways("x", other, other)
    far0 = shift(up0, "x", 1)
    far1 = shift(down1, "x", -1)

    acts = [act, other, up0, down0, up1, down1, far0, far1]
    outs = second(pos, acts, own, peer, count)
    acts_own, acts_peer = outs[0:2]
    up, down, keep = outs[2:6], outs[6:10], outs[10]
    send_up, send_down = up[0], down[0]
    for s in range(1, 4):
        got_up, got_down = shift(send_up, "z", 1), shift(send_down, "z", -1)
        if s == 1:
            acts_peer = shift(acts_peer, "core", 1)
        elif s == 2:
            grad_w_in = win_grad(
                rows, rows_peer, acts_own, after(acts_peer, send_up, send_down), mask_in
            )
            got_up, got_down, _ = lax.optimization_barrier((got_up, got_down, grad_w_in))
        n = two if s < 3 else count
        send_up = (up[s] + f(got_up[:n])).astype(BF)
        send_down = (down[s] + f(got_down[:n])).astype(BF)
    end_up, end_down = shift(send_up, "z", 1), shift(send_down, "z", -1)
    send = (keep[count:] + f(got_up[count:]) + f(end_down)).astype(BF)
    mine = keep[:count] + f(got_down[count:]) + f(end_up)
    grad_inputs = (mine + f(shift(send, "ylo", 1))).astype(BF)
    return grad_inputs, grad_w_in, grad_w_out


def solution(mesh):
    fine = Mesh(mesh.devices.reshape(2, 4, 8, 2, 2), ("yhi", "x", "z", "ylo", "core"))
    row, col = ("yhi", "x"), ("z", "ylo", "core")
    return jax.shard_map(
        body,
        mesh=fine,
        in_specs=(
            P(col, row),
            P(col, row),
            P(row, col),
            P(row, col),
            P(col, row),
            P(row, col),
            P(col, row),
        ),
        out_specs=(P(col, row), P(row, col), P(col, row)),
        check_vma=False,
    )
```

```python
import functools
import math

import jax
import jax.numpy as jnp
from jax import lax
from jax.experimental import pallas as pl
from jax.experimental.pallas import tpu as pltpu
from jax.sharding import Mesh
from jax.sharding import PartitionSpec as P

coef = math.sqrt(2.0 / math.pi)
VMEM = 16
BF = jnp.bfloat16
F32 = jnp.float32
SIZE = {"yhi": 2, "x": 4, "z": 8, "ylo": 2, "core": 2}
TO_X = (
    (2, 1, BF),
    (-1, 1, BF),
    (1, 1, F32),
    (2, 0, BF),
    (1, 0, BF),
    (-1, 0, F32),
    (0, 0, F32),
    (0, 1, F32),
)
FROM_X = ((0, 0), (0, 1), (-1, 0), (1, 0), (-1, 1), (1, 1), (2, 0), (2, 1))
NT = (((1,), (1,)), ((), ()))
TN = (((0,), (0,)), ((), ()))
MIB = 1 << 20


def shift(value, axis, by):
    count = SIZE[axis]
    return lax.ppermute(value, axis, [(i, (i + by) % count) for i in range(count)])


def params(mib):
    return pltpu.CompilerParams(vmem_limit_bytes=mib * MIB)


def cost(flops, size):
    return pl.CostEstimate(flops=flops, bytes_accessed=size, transcendentals=0)


def after(value, *others):
    return lax.optimization_barrier((value, *others))[0]


def together(*values):
    return lax.optimization_barrier(values)


def both_ways(axis, up, down):
    return shift(up, axis, 1), shift(down, axis, -1)


def plan_z():
    both = lambda off: [(0, off, 0), (32, off, 1), (64, off, 2)]
    plan = [both(0)]
    for step in range(1, 4):
        plan += [both(-step), both(step)]
    return plan + [[(0, 4, 0), (32, 4, 1)], [(0, 4, 2)]]


def plan_x(count):
    both = lambda off: [(0, off, 0), (count, off, 1)]
    return [both(0), both(-1), both(1), both(2)]


def whole(shape):
    return pl.BlockSpec(shape, lambda *_: (0,) * len(shape))


def place_z(pos, off, half):
    owner = lax.rem(pos[2] + (off + 8), 8)
    return pl.ds(pl.multiple_of(half * 256 + owner * 32, 32), 32)


def place_x(pos, off, y):
    owner = lax.rem(pos[0] + y, 2) * 4 + lax.rem(pos[1] + (off + 4), 4)
    return [pl.ds(pl.multiple_of(half * 256 + owner * 32, 32), 32) for half in range(2)]


def in_vmem(count):
    return [pl.BlockSpec(memory_space=pltpu.VMEM)] * count


def call(kernel, name, pos, arrays, shapes, scratch, flops):
    return pl.pallas_call(
        kernel,
        in_specs=[pl.BlockSpec(memory_space=pltpu.SMEM)] + in_vmem(len(arrays)),
        out_specs=in_vmem(len(shapes)),
        out_shape=[jax.ShapeDtypeStruct(n, t) for n, t in shapes],
        scratch_shapes=scratch,
        compiler_params=params(VMEM),
        cost_estimate=cost(flops, MIB),
        name=name,
    )(pos, *arrays)


def kept(mask, row, col, values):
    return jnp.where(mask[row, col] > 0, values, jnp.zeros_like(values))


def mask_kernel(mask_out, mask_in, w_out, w_in, theirs, out):
    out[1536:1600, 0:768] = theirs[...]
    out[1536:1600, 768:1536] = theirs[...]

    @pl.loop(0, 6)
    def _(i):
        rows = pl.ds(pl.multiple_of(i * 128, 128), 128)
        later = pl.ds(pl.multiple_of(i * 128 + 768, 128), 128)
        for j in range(12):
            cols = slice(j * 128, j * 128 + 128)
            out[rows, cols] = kept(mask_out, i, j, w_out[rows, cols])
            side, tile = j // 6, j % 6
            source = pl.ds(pl.multiple_of(i * 128 + side * 768, 128), 128)
            part = w_in[source, tile * 128 : tile * 128 + 128]
            out[later, cols] = kept(mask_in, i + side * 6, tile, part)


def masked(mask_out, mask_in, w_out, w_in, theirs):
    return pl.pallas_call(
        mask_kernel,
        in_specs=[pl.BlockSpec(memory_space=pltpu.SMEM)] * 2 + in_vmem(3),
        out_specs=pl.BlockSpec(memory_space=pltpu.VMEM),
        out_shape=jax.ShapeDtypeStruct((1600, 1536), BF),
        compiler_params=params(VMEM),
        cost_estimate=cost(0, 4 * MIB),
        name="masked",
    )(mask_out, mask_in, w_out, w_in, theirs)


def values_kernel(pos, pre, hidden, slopes, other):
    core = pos[4]
    zval = pre[...].astype(F32)
    tval = jnp.tanh(coef * (zval + 0.044715 * zval**3))
    hidden[...] = (0.5 * zval * (1.0 + tval)).astype(BF)
    for half in range(2):
        first = lax.rem(pos[3] + half, 2) * 64
        mine = pl.ds(pl.multiple_of(first + core * 32, 32), 32)
        theirs = pl.ds(pl.multiple_of(first + (1 - core) * 32, 32), 32)
        rows = slice(half * 32, half * 32 + 32)
        slopes[rows, :] = slope(pre[mine, :])
        other[rows, :] = pre[theirs, :]


def first_kernel(plan, pos, *refs):
    pieces = refs[: len(plan)]
    own_ref, peer_ref, rows, ins = refs[len(plan) : len(plan) + 4]
    outs, held = refs[len(plan) + 4 : -1], refs[-1]
    for ref, spots in zip(pieces, plan):
        for first, off, half in spots:
            rows[place_z(pos, off, half), :] = ref[first : first + 32, :]
            if half == 2:
                ins[place_z(pos, off, 0), :] = ref[first : first + 32, :]

    for half, weight in enumerate((own_ref, peer_ref)):
        held[...] = lax.dot_general(
            rows[0:512, :], weight[0:768, :], NT, preferred_element_type=F32
        )
        where = slice(half * 768, half * 768 + 768)

        for ref, (off, y, _) in zip(outs, TO_X):
            for k, place in enumerate(place_x(pos, off, y)):
                ref[k * 32 : k * 32 + 32, where] = held[place, :].astype(ref.dtype)


def first(pos, pieces, own, peer):
    heights = [(768, BF), (256, BF)] + [(64, kind) for _, _, kind in TO_X]
    return call(
        functools.partial(first_kernel, plan_z()),
        "first",
        pos,
        [*pieces, own, peer],
        [((n, 1536), t) for n, t in heights],
        [pltpu.VMEM((512, 768), F32)],
        4 * 512 * 1536 * 1536,
    )


def second_kernel(pos, *refs):
    pieces, refs = refs[: len(FROM_X)], refs[len(FROM_X) :]
    in_other, own_ref, peer_ref, rows, pack = refs[:5]
    outs = refs[5:-2]
    rows_peer, held = refs[-2:]
    for ref, (off, y) in zip(pieces, FROM_X):
        for k, place in enumerate(place_x(pos, off, y)):
            at = slice(k * 32, k * 32 + 32)
            rows[place, :] = ref[at, 0:768]
            rows_peer[place, :] = ref[at, 768:1536]
    pack[0:256, :] = in_other[...]
    pack[256:512, 0:768] = rows_peer[0:256, :]
    pack[256:512, 768:1536] = rows_peer[256:512, :]

    for step in range(2):
        where = slice(step * 768, step * 768 + 768)
        out = lax.dot_general(rows[...], own_ref[768:1536, where], NT, preferred_element_type=F32)
        out += lax.dot_general(
            rows_peer[...], peer_ref[768:1536, where], NT, preferred_element_type=F32
        )
        held[...] = out

        def put(ref, at, off, half):
            ref[at : at + 32, where] = held[place_z(pos, off, half), :].astype(ref.dtype)

        up, down, keep = outs[0:4], outs[4:8], outs[8]
        for s in range(4):
            put(up[s], 0, 4 - s, 0)
            put(down[s], 0, s - 4, 1)
            if s < 3:
                put(up[s], 32, 3 - s, 1)
                put(down[s], 32, s - 3, 0)
        put(keep, 0, 0, 0)
        put(keep, 32, 0, 1)


def second(pos, pieces, in_other, own, peer):
    ring = [(64, BF), (64, F32), (64, F32), (32, F32)]
    shapes = [((512, 768), BF), ((512, 1536), BF)]
    shapes += [((n, 1536), t) for n, t in ring + ring + [(64, F32)]]
    return call(
        second_kernel,
        "second",
        pos,
        [*pieces, in_other, own, peer],
        shapes,
        [pltpu.VMEM((512, 768), BF), pltpu.VMEM((512, 768), F32)],
        4 * 512 * 1536 * 1536,
    )


def store_kept(total, mask, first, out):
    for i in range(out.shape[0] // 128):
        rows = slice(i * 128, i * 128 + 128)
        for j in range(out.shape[1] // 128):
            cols = slice(j * 128, j * 128 + 128)
            out[rows, cols] = kept(mask, first + i, j, total[rows, cols]).astype(BF)


def wout_kernel(plan, pos, mask, *refs):
    pieces = refs[: len(plan)]
    own, peer, out, held = refs[len(plan) :]
    for ref, spots in zip(pieces, plan):
        for first, off, half in spots:
            owner = lax.rem(pos[0] + half, 2) * 4 + lax.rem(pos[1] + (off + 4), 4)
            held[owner] = ref[first : first + 128, :].reshape(2, 2, 32, -1)
    total = None
    for k, part in enumerate((own, peer)):
        core = lax.rem(pos[4] + k, 2)
        halves = [held[:, lax.rem(pos[3] + y, 2), core].reshape(256, -1) for y in range(2)]
        left = jnp.concatenate(halves)
        term = lax.dot_general(left, part[0:512, :], TN, preferred_element_type=F32)
        total = term if total is None else total + term
    store_kept(total, mask, pl.program_id(0) * (out.shape[0] // 128), out)


def wout_grad(pos, pieces, own, peer, mask):
    block = 384
    return pl.pallas_call(
        functools.partial(wout_kernel, plan_x(128)),
        grid_spec=pltpu.PrefetchScalarGridSpec(
            num_scalar_prefetch=2,
            grid=(768 // block,),
            in_specs=[pl.BlockSpec((a.shape[0], block), lambda i, *_: (0, i)) for a in pieces]
            + in_vmem(2),
            out_specs=pl.BlockSpec((block, 1536), lambda i, *_: (i, 0)),
            scratch_shapes=[pltpu.VMEM((8, 2, 2, 32, block), BF)],
        ),
        out_shape=jax.ShapeDtypeStruct((768, 1536), BF),
        compiler_params=params(VMEM),
        cost_estimate=cost(4 * 1024 * 1536 * 768, 8 * MIB),
        name="wout_grad",
    )(pos, mask, *pieces, own, peer)


def win_kernel(mask, in0, in1, peer0, peer1, acts, peer, out):
    left = jnp.concatenate([in0[...], in1[...]])
    total = lax.dot_general(left, acts[...], TN, preferred_element_type=F32)
    left = jnp.concatenate([peer0[...], peer1[...]])
    right = jnp.concatenate([peer[256:512, 0:768], peer[256:512, 768:1536]])
    total += lax.dot_general(left, right, TN, preferred_element_type=F32)
    store_kept(total, mask, pl.program_id(0) * (out.shape[0] // 128), out)


def win_grad(rows, pack, rows_peer, pack_peer, acts, mask):
    block = 768
    at = lambda k: pl.BlockSpec((256, block), lambda i, _: (k, i))
    return pl.pallas_call(
        win_kernel,
        grid_spec=pltpu.PrefetchScalarGridSpec(
            num_scalar_prefetch=1,
            grid=(1536 // block,),
            in_specs=[at(2), at(0), at(2), at(0)] + in_vmem(2),
            out_specs=pl.BlockSpec((block, 768), lambda i, _: (i, 0)),
        ),
        out_shape=jax.ShapeDtypeStruct((1536, 768), BF),
        compiler_params=params(VMEM),
        cost_estimate=cost(4 * 1024 * 1536 * 768, 8 * MIB),
        name="win_grad",
    )(mask, rows, pack, rows_peer, pack_peer, acts, pack_peer)


def slope(values):
    zval = values.astype(F32)
    tval = jnp.tanh(coef * (zval + 0.044715 * zval**3))
    return 0.5 * (1.0 + tval) + 0.5 * zval * (1.0 - tval * tval) * coef * (
        1.0 + 3.0 * 0.044715 * zval * zval
    )


def body(inputs, grad_out, pre_act, w_in, w_out, mask_in, mask_out):
    names = ("yhi", "x", "z", "ylo", "core")
    pos = jnp.stack([lax.axis_index(n) for n in names]).astype(jnp.int32)
    f = lambda v: v.astype(F32)
    count, two = 32, 64

    other = shift(grad_out, "ylo", 1)
    shapes = [((128, 768), BF), ((64, 768), F32), ((64, 768), BF)]
    hidden, slopes, theirs = call(values_kernel, "values", pos, [pre_act], shapes, [], MIB)
    hidden_other = shift(hidden, "yhi", 1)
    other, hidden, theirs = together(other, hidden, theirs)
    sent = jnp.concatenate([grad_out, other, inputs])
    up1, down1 = both_ways("z", sent, sent)
    own = masked(after(mask_out, sent), mask_in, w_out, w_in, theirs)
    up1, down1, own, hidden_other = together(up1, down1, own, hidden_other)
    up2, down2 = both_ways("z", up1, down1)
    peer = shift(own, "core", 1)
    hid = jnp.concatenate([hidden, hidden_other])
    hid_up, hid_down = both_ways("x", hid, hid)
    up2, down2 = together(up2, down2)
    up3, down3 = both_ways("z", up2, down2)
    up3, down3, hid_up, hid_down = together(up3, down3, hid_up, hid_down)
    up4, down4 = both_ways("z", up3[:64], down3[64:])
    hid_far = shift(after(hid_up, up3), "x", 1)
    up4, down4, hid_far = together(up4, down4, hid_far)
    pieces = [sent, up1, down1, up2, down2, up3, down3, up4, down4]

    rows, ins, far1, down1, up1, far0, up0, down0, keep0, keep1 = first(pos, pieces, own, peer)
    got, down1 = both_ways("x", far1, down1)
    in_other = shift(ins, "ylo", 1)
    slopes = jnp.concatenate([slopes, slope(after(peer, keep1)[1536:, :768])], axis=1)
    rows_peer = shift(after(rows, slopes), "core", 1)
    got, down1, slopes = together(got, down1, slopes)
    up1, got = both_ways("x", (up1 + f(got)).astype(BF), far0)
    up1, got, in_other = together(up1, got, in_other)
    other = shift((keep1 + f(down1) + f(up1)).astype(BF), "yhi", 1)
    up0, down0 = both_ways("x", up0, (down0 + f(got)).astype(BF))
    act = ((keep0 + f(up0) + f(down0) + f(other)) * slopes).astype(BF)

    other = shift(act, "yhi", 1)
    up0, down0 = both_ways("x", act, act)
    hidden_pieces = [hid, hid_up, hid_down, hid_far]
    grad_w_out = wout_grad(pos, hidden_pieces, rows, after(rows_peer, act), mask_out)
    other, up0, down0, grad_w_out = together(other, up0, down0, grad_w_out)
    up1, down1 = both_ways("x", other, other)
    far0 = shift(up0, "x", 1)
    far1 = shift(down1, "x", -1)

    acts = [act, other, up0, down0, up1, down1, far0, far1]
    outs = second(pos, acts, in_other, own, peer)
    acts, pack = outs[0:2]
    up, down, keep = outs[2:6], outs[6:10], outs[10]
    send_up, send_down = up[0], down[0]
    for s in range(1, 4):
        got_up, got_down = shift(send_up, "z", 1), shift(send_down, "z", -1)
        if s == 1:
            pack_peer = shift(pack, "core", 1)
        elif s == 2:
            grad_w_in = win_grad(
                rows, pack, rows_peer, after(pack_peer, send_up, send_down), acts, mask_in
            )
            got_up, got_down, _ = lax.optimization_barrier((got_up, got_down, grad_w_in))
        n = two if s < 3 else count
        send_up = (up[s] + f(got_up[:n])).astype(BF)
        send_down = (down[s] + f(got_down[:n])).astype(BF)
    end_up, end_down = shift(send_up, "z", 1), shift(send_down, "z", -1)
    send = (keep[count:] + f(got_up[count:]) + f(end_down)).astype(BF)
    mine = keep[:count] + f(got_down[count:]) + f(end_up)
    grad_inputs = (mine + f(shift(send, "ylo", 1))).astype(BF)
    return grad_inputs, grad_w_in, grad_w_out


def solution(mesh):
    fine = Mesh(mesh.devices.reshape(2, 4, 8, 2, 2), ("yhi", "x", "z", "ylo", "core"))
    row, col = ("yhi", "x"), ("z", "ylo", "core")
    return jax.shard_map(
        body,
        mesh=fine,
        in_specs=(
            P(col, row),
            P(col, row),
            P(row, col),
            P(row, col),
            P(col, row),
            P(row, col),
            P(col, row),
        ),
        out_specs=(P(col, row), P(row, col), P(col, row)),
        check_vma=False,
    )
```

```python
import functools
import math

import jax
import jax.numpy as jnp
from jax import lax
from jax.experimental import pallas as pl
from jax.experimental.pallas import tpu as pltpu
from jax.sharding import Mesh
from jax.sharding import PartitionSpec as P

coef = math.sqrt(2.0 / math.pi)
VMEM = 16
BF = jnp.bfloat16
F32 = jnp.float32
SIZE = {"yhi": 2, "x": 4, "z": 8, "ylo": 2, "core": 2}
TO_X = (
    (2, 1, BF),
    (-1, 1, BF),
    (1, 1, F32),
    (2, 0, BF),
    (1, 0, BF),
    (-1, 0, F32),
    (0, 0, F32),
    (0, 1, F32),
)
FROM_X = ((0, 0), (0, 1), (-1, 0), (1, 0), (-1, 1), (1, 1), (2, 0), (2, 1))
NT = (((1,), (1,)), ((), ()))
TN = (((0,), (0,)), ((), ()))
MIB = 1 << 20


def shift(value, axis, by):
    count = SIZE[axis]
    return lax.ppermute(value, axis, [(i, (i + by) % count) for i in range(count)])


def params(mib):
    return pltpu.CompilerParams(vmem_limit_bytes=mib * MIB)


def cost(flops, size):
    return pl.CostEstimate(flops=flops, bytes_accessed=size, transcendentals=0)


def after(value, *others):
    return lax.optimization_barrier((value, *others))[0]


def together(*values):
    return lax.optimization_barrier(values)


def both_ways(axis, up, down):
    return shift(up, axis, 1), shift(down, axis, -1)


def plan_z():
    both = lambda off: [(0, off, 0), (32, off, 1), (64, off, 2)]
    plan = [both(0)]
    for step in range(1, 4):
        plan += [both(-step), both(step)]
    return plan + [[(0, 4, 0), (32, 4, 1)], [(0, 4, 2)]]


def plan_x(count):
    both = lambda off: [(0, off, 0), (count, off, 1)]
    return [both(0), both(-1), both(1), both(2)]


def whole(shape):
    return pl.BlockSpec(shape, lambda *_: (0,) * len(shape))


def place_z(pos, off, half):
    owner = lax.rem(pos[2] + (off + 8), 8)
    return pl.ds(pl.multiple_of(half * 256 + owner * 32, 32), 32)


def place_x(pos, off, y):
    owner = lax.rem(pos[0] + y, 2) * 4 + lax.rem(pos[1] + (off + 4), 4)
    return [pl.ds(pl.multiple_of(half * 256 + owner * 32, 32), 32) for half in range(2)]


def in_vmem(count):
    return [pl.BlockSpec(memory_space=pltpu.VMEM)] * count


def call(kernel, name, pos, arrays, shapes, scratch, flops):
    return pl.pallas_call(
        kernel,
        in_specs=[pl.BlockSpec(memory_space=pltpu.SMEM)] + in_vmem(len(arrays)),
        out_specs=in_vmem(len(shapes)),
        out_shape=[jax.ShapeDtypeStruct(n, t) for n, t in shapes],
        scratch_shapes=scratch,
        compiler_params=params(VMEM),
        cost_estimate=cost(flops, MIB),
        name=name,
    )(pos, *arrays)


def kept(mask, row, col, values):
    return jnp.where(mask[row, col] > 0, values, jnp.zeros_like(values))


def mask_kernel(mask_out, mask_in, w_out, w_in, theirs, out):
    out[1536:1600, 0:768] = theirs[...]
    out[1536:1600, 768:1536] = theirs[...]

    @pl.loop(0, 6)
    def _(i):
        rows = pl.ds(pl.multiple_of(i * 128, 128), 128)
        later = pl.ds(pl.multiple_of(i * 128 + 768, 128), 128)
        for j in range(12):
            cols = slice(j * 128, j * 128 + 128)
            out[rows, cols] = kept(mask_out, i, j, w_out[rows, cols])
            side, tile = j // 6, j % 6
            source = pl.ds(pl.multiple_of(i * 128 + side * 768, 128), 128)
            part = w_in[source, tile * 128 : tile * 128 + 128]
            out[later, cols] = kept(mask_in, i + side * 6, tile, part)


def masked(mask_out, mask_in, w_out, w_in, theirs):
    return pl.pallas_call(
        mask_kernel,
        in_specs=[pl.BlockSpec(memory_space=pltpu.SMEM)] * 2 + in_vmem(3),
        out_specs=pl.BlockSpec(memory_space=pltpu.VMEM),
        out_shape=jax.ShapeDtypeStruct((1600, 1536), BF),
        compiler_params=params(VMEM),
        cost_estimate=cost(0, 4 * MIB),
        name="masked",
    )(mask_out, mask_in, w_out, w_in, theirs)


def values_kernel(pos, pre, hidden, slopes, other):
    core = pos[4]
    zval = pre[...].astype(F32)
    tval = jnp.tanh(coef * (zval + 0.044715 * zval**3))
    hidden[...] = (0.5 * zval * (1.0 + tval)).astype(BF)
    for half in range(2):
        first = lax.rem(pos[3] + half, 2) * 64
        mine = pl.ds(pl.multiple_of(first + core * 32, 32), 32)
        theirs = pl.ds(pl.multiple_of(first + (1 - core) * 32, 32), 32)
        rows = slice(half * 32, half * 32 + 32)
        slopes[rows, :] = slope(pre[mine, :])
        other[rows, :] = pre[theirs, :]


def first_kernel(plan, pos, *refs):
    pieces = refs[: len(plan)]
    own_ref, peer_ref, rows, ins0, ins1 = refs[len(plan) : len(plan) + 5]
    outs, held = refs[len(plan) + 5 : -1], refs[-1]
    for ref, spots in zip(pieces, plan):
        for first, off, half in spots:
            rows[place_z(pos, off, half), :] = ref[first : first + 32, :]

    ins0[...] = rows[512:640, :]
    ins1[...] = rows[640:768, :]

    for half, weight in enumerate((own_ref, peer_ref)):
        held[...] = lax.dot_general(
            rows[0:512, :], weight[0:768, :], NT, preferred_element_type=F32
        )
        where = slice(half * 768, half * 768 + 768)

        for ref, (off, y, _) in zip(outs, TO_X):
            for k, place in enumerate(place_x(pos, off, y)):
                ref[k * 32 : k * 32 + 32, where] = held[place, :].astype(ref.dtype)


def first(pos, pieces, own, peer):
    heights = [(768, BF), (128, BF), (128, BF)] + [(64, kind) for _, _, kind in TO_X]
    return call(
        functools.partial(first_kernel, plan_z()),
        "first",
        pos,
        [*pieces, own, peer],
        [((n, 1536), t) for n, t in heights],
        [pltpu.VMEM((512, 768), F32)],
        4 * 512 * 1536 * 1536,
    )


def second_kernel(pos, *refs):
    pieces, refs = refs[: len(FROM_X)], refs[len(FROM_X) :]
    in_other0, in_other1, own_ref, peer_ref, rows, pack = refs[:6]
    outs = refs[6:-2]
    rows_peer, held = refs[-2:]
    for ref, (off, y) in zip(pieces, FROM_X):
        for k, place in enumerate(place_x(pos, off, y)):
            at = slice(k * 32, k * 32 + 32)
            rows[place, :] = ref[at, 0:768]
            rows_peer[place, :] = ref[at, 768:1536]
    pack[0:128, :] = in_other0[...]
    pack[128:256, :] = in_other1[...]
    pack[256:512, 0:768] = rows_peer[0:256, :]
    pack[256:512, 768:1536] = rows_peer[256:512, :]

    for step in range(2):
        where = slice(step * 768, step * 768 + 768)
        out = lax.dot_general(rows[...], own_ref[768:1536, where], NT, preferred_element_type=F32)
        out += lax.dot_general(
            rows_peer[...], peer_ref[768:1536, where], NT, preferred_element_type=F32
        )
        held[...] = out

        def put(ref, at, off, half):
            ref[at : at + 32, where] = held[place_z(pos, off, half), :].astype(ref.dtype)

        up, down, keep = outs[0:4], outs[4:8], outs[8]
        for s in range(4):
            put(up[s], 0, 4 - s, 0)
            put(down[s], 0, s - 4, 1)
            if s < 3:
                put(up[s], 32, 3 - s, 1)
                put(down[s], 32, s - 3, 0)
        put(keep, 0, 0, 0)
        put(keep, 32, 0, 1)


def second(pos, pieces, in_other, own, peer):
    ring = [(64, BF), (64, F32), (64, F32), (32, F32)]
    shapes = [((512, 768), BF), ((512, 1536), BF)]
    shapes += [((n, 1536), t) for n, t in ring + ring + [(64, F32)]]
    return call(
        second_kernel,
        "second",
        pos,
        [*pieces, *in_other, own, peer],
        shapes,
        [pltpu.VMEM((512, 768), BF), pltpu.VMEM((512, 768), F32)],
        4 * 512 * 1536 * 1536,
    )


def store_kept(total, mask, first, out):
    for i in range(out.shape[0] // 128):
        rows = slice(i * 128, i * 128 + 128)
        for j in range(out.shape[1] // 128):
            cols = slice(j * 128, j * 128 + 128)
            out[rows, cols] = kept(mask, first + i, j, total[rows, cols]).astype(BF)


def wout_kernel(plan, pos, mask, *refs):
    pieces = refs[: len(plan)]
    own, peer, out, held = refs[len(plan) :]
    for ref, spots in zip(pieces, plan):
        for first, off, half in spots:
            owner = lax.rem(pos[0] + half, 2) * 4 + lax.rem(pos[1] + (off + 4), 4)
            held[owner] = ref[first : first + 128, :].reshape(2, 2, 32, -1)
    total = None
    for k, part in enumerate((own, peer)):
        core = lax.rem(pos[4] + k, 2)
        halves = [held[:, lax.rem(pos[3] + y, 2), core].reshape(256, -1) for y in range(2)]
        left = jnp.concatenate(halves)
        term = lax.dot_general(left, part[0:512, :], TN, preferred_element_type=F32)
        total = term if total is None else total + term
    store_kept(total, mask, pl.program_id(0) * (out.shape[0] // 128), out)


def wout_grad(pos, pieces, own, peer, mask):
    block = 384
    return pl.pallas_call(
        functools.partial(wout_kernel, plan_x(128)),
        grid_spec=pltpu.PrefetchScalarGridSpec(
            num_scalar_prefetch=2,
            grid=(768 // block,),
            in_specs=[pl.BlockSpec((a.shape[0], block), lambda i, *_: (0, i)) for a in pieces]
            + in_vmem(2),
            out_specs=pl.BlockSpec((block, 1536), lambda i, *_: (i, 0)),
            scratch_shapes=[pltpu.VMEM((8, 2, 2, 32, block), BF)],
        ),
        out_shape=jax.ShapeDtypeStruct((768, 1536), BF),
        compiler_params=params(VMEM),
        cost_estimate=cost(4 * 1024 * 1536 * 768, 8 * MIB),
        name="wout_grad",
    )(pos, mask, *pieces, own, peer)


def win_kernel(mask, in0, in1, peer0, peer1, acts, peer, out):
    left = jnp.concatenate([in0[...], in1[...]])
    total = lax.dot_general(left, acts[...], TN, preferred_element_type=F32)
    left = jnp.concatenate([peer0[...], peer1[...]])
    right = jnp.concatenate([peer[256:512, 0:768], peer[256:512, 768:1536]])
    total += lax.dot_general(left, right, TN, preferred_element_type=F32)
    store_kept(total, mask, pl.program_id(0) * (out.shape[0] // 128), out)


def win_grad(rows, pack, rows_peer, pack_peer, acts, mask):
    block = 768
    at = lambda k: pl.BlockSpec((256, block), lambda i, _: (k, i))
    return pl.pallas_call(
        win_kernel,
        grid_spec=pltpu.PrefetchScalarGridSpec(
            num_scalar_prefetch=1,
            grid=(1536 // block,),
            in_specs=[at(2), at(0), at(2), at(0)] + in_vmem(2),
            out_specs=pl.BlockSpec((block, 768), lambda i, _: (i, 0)),
        ),
        out_shape=jax.ShapeDtypeStruct((1536, 768), BF),
        compiler_params=params(VMEM),
        cost_estimate=cost(4 * 1024 * 1536 * 768, 8 * MIB),
        name="win_grad",
    )(mask, rows, pack, rows_peer, pack_peer, acts, pack_peer)


def slope(values):
    zval = values.astype(F32)
    tval = jnp.tanh(coef * (zval + 0.044715 * zval**3))
    return 0.5 * (1.0 + tval) + 0.5 * zval * (1.0 - tval * tval) * coef * (
        1.0 + 3.0 * 0.044715 * zval * zval
    )


def body(inputs, grad_out, pre_act, w_in, w_out, mask_in, mask_out):
    names = ("yhi", "x", "z", "ylo", "core")
    pos = jnp.stack([lax.axis_index(n) for n in names]).astype(jnp.int32)
    f = lambda v: v.astype(F32)
    count, two = 32, 64

    other = shift(grad_out, "ylo", 1)
    shapes = [((128, 768), BF), ((64, 768), F32), ((64, 768), BF)]
    hidden, slopes, theirs = call(values_kernel, "values", pos, [pre_act], shapes, [], MIB)
    hidden_other = shift(hidden, "yhi", 1)
    other, hidden, theirs = together(other, hidden, theirs)
    sent = jnp.concatenate([grad_out, other, inputs])
    up1, down1 = both_ways("z", sent, sent)
    own = masked(after(mask_out, sent), mask_in, w_out, w_in, theirs)
    up1, down1, own, hidden_other = together(up1, down1, own, hidden_other)
    up2, down2 = both_ways("z", up1, down1)
    peer = shift(own, "core", 1)
    hid = jnp.concatenate([hidden, hidden_other])
    hid_up, hid_down = both_ways("x", hid, hid)
    up2, down2 = together(up2, down2)
    up3, down3 = both_ways("z", up2, down2)
    up3, down3, hid_up, hid_down = together(up3, down3, hid_up, hid_down)
    up4, down4 = both_ways("z", up3[:64], down3[64:])
    hid_far = shift(after(hid_up, up3), "x", 1)
    up4, down4, hid_far = together(up4, down4, hid_far)
    pieces = [sent, up1, down1, up2, down2, up3, down3, up4, down4]

    rows, ins0, ins1, far1, down1, up1, far0, up0, down0, keep0, keep1 = first(pos, pieces, own, peer)
    got, down1 = both_ways("x", far1, down1)
    in_other = shift(ins0, "ylo", 1)
    slopes = jnp.concatenate([slopes, slope(after(peer, keep1)[1536:, :768])], axis=1)
    rows_peer = shift(after(rows, slopes), "core", 1)
    got, down1, slopes = together(got, down1, slopes)
    up1, got = both_ways("x", (up1 + f(got)).astype(BF), far0)
    up1, got, in_other = together(up1, got, in_other)
    other = shift((keep1 + f(down1) + f(up1)).astype(BF), "yhi", 1)
    up0, down0 = both_ways("x", up0, (down0 + f(got)).astype(BF))
    act = ((keep0 + f(up0) + f(down0) + f(other)) * slopes).astype(BF)

    other = shift(act, "yhi", 1)
    up0, down0 = both_ways("x", act, act)
    hidden_pieces = [hid, hid_up, hid_down, hid_far]
    grad_w_out = wout_grad(pos, hidden_pieces, rows, after(rows_peer, act), mask_out)
    other, up0, down0, grad_w_out = together(other, up0, down0, grad_w_out)
    up1, down1 = both_ways("x", other, other)
    in_other = [in_other, shift(after(ins1, other), "ylo", 1)]
    far0 = shift(up0, "x", 1)
    far1 = shift(down1, "x", -1)

    acts = [act, other, up0, down0, up1, down1, far0, far1]
    outs = second(pos, acts, in_other, own, peer)
    acts, pack = outs[0:2]
    up, down, keep = outs[2:6], outs[6:10], outs[10]
    send_up, send_down = up[0], down[0]
    for s in range(1, 4):
        got_up, got_down = shift(send_up, "z", 1), shift(send_down, "z", -1)
        if s == 1:
            pack_peer = shift(pack, "core", 1)
        elif s == 2:
            grad_w_in = win_grad(
                rows, pack, rows_peer, after(pack_peer, send_up, send_down), acts, mask_in
            )
            got_up, got_down, _ = lax.optimization_barrier((got_up, got_down, grad_w_in))
        n = two if s < 3 else count
        send_up = (up[s] + f(got_up[:n])).astype(BF)
        send_down = (down[s] + f(got_down[:n])).astype(BF)
    end_up, end_down = shift(send_up, "z", 1), shift(send_down, "z", -1)
    send = (keep[count:] + f(got_up[count:]) + f(end_down)).astype(BF)
    mine = keep[:count] + f(got_down[count:]) + f(end_up)
    grad_inputs = (mine + f(shift(send, "ylo", 1))).astype(BF)
    return grad_inputs, grad_w_in, grad_w_out


def solution(mesh):
    fine = Mesh(mesh.devices.reshape(2, 4, 8, 2, 2), ("yhi", "x", "z", "ylo", "core"))
    row, col = ("yhi", "x"), ("z", "ylo", "core")
    return jax.shard_map(
        body,
        mesh=fine,
        in_specs=(
            P(col, row),
            P(col, row),
            P(row, col),
            P(row, col),
            P(col, row),
            P(row, col),
            P(col, row),
        ),
        out_specs=(P(col, row), P(row, col), P(col, row)),
        check_vma=False,
    )
```

```python
import functools
import math

import jax
import jax.numpy as jnp
from jax import lax
from jax.experimental import pallas as pl
from jax.experimental.pallas import tpu as pltpu
from jax.sharding import Mesh
from jax.sharding import PartitionSpec as P

coef = math.sqrt(2.0 / math.pi)
VMEM = 16
BF = jnp.bfloat16
F32 = jnp.float32
SIZE = {"yhi": 2, "x": 4, "z": 8, "ylo": 2, "core": 2}
TO_X = (
    (2, 1, BF),
    (-1, 1, BF),
    (1, 1, F32),
    (2, 0, BF),
    (1, 0, BF),
    (-1, 0, F32),
    (0, 0, F32),
    (0, 1, F32),
)
FROM_X = ((0, 0), (0, 1), (-1, 0), (1, 0), (-1, 1), (1, 1), (2, 0), (2, 1))
NT = (((1,), (1,)), ((), ()))
TN = (((0,), (0,)), ((), ()))
MIB = 1 << 20


def shift(value, axis, by):
    count = SIZE[axis]
    return lax.ppermute(value, axis, [(i, (i + by) % count) for i in range(count)])


def params(mib):
    return pltpu.CompilerParams(vmem_limit_bytes=mib * MIB)


def cost(flops, size):
    return pl.CostEstimate(flops=flops, bytes_accessed=size, transcendentals=0)


def after(value, *others):
    return lax.optimization_barrier((value, *others))[0]


def together(*values):
    return lax.optimization_barrier(values)


def both_ways(axis, up, down):
    return shift(up, axis, 1), shift(down, axis, -1)


def plan_z():
    both = lambda off: [(0, off, 0), (32, off, 1), (64, off, 2)]
    plan = [both(0)]
    for step in range(1, 4):
        plan += [both(-step), both(step)]
    return plan + [[(0, 4, 0), (32, 4, 1)], [(0, 4, 2)]]


def plan_x(count):
    both = lambda off: [(0, off, 0), (count, off, 1)]
    return [both(0), both(-1), both(1), both(2)]


def whole(shape):
    return pl.BlockSpec(shape, lambda *_: (0,) * len(shape))


def place_z(pos, off, half):
    owner = lax.rem(pos[2] + (off + 8), 8)
    return pl.ds(pl.multiple_of(half * 256 + owner * 32, 32), 32)


def place_x(pos, off, y):
    owner = lax.rem(pos[0] + y, 2) * 4 + lax.rem(pos[1] + (off + 4), 4)
    return [pl.ds(pl.multiple_of(half * 256 + owner * 32, 32), 32) for half in range(2)]


def in_vmem(count):
    return [pl.BlockSpec(memory_space=pltpu.VMEM)] * count


def call(kernel, name, pos, arrays, shapes, scratch, flops):
    return pl.pallas_call(
        kernel,
        in_specs=[pl.BlockSpec(memory_space=pltpu.SMEM)] + in_vmem(len(arrays)),
        out_specs=in_vmem(len(shapes)),
        out_shape=[jax.ShapeDtypeStruct(n, t) for n, t in shapes],
        scratch_shapes=scratch,
        compiler_params=params(VMEM),
        cost_estimate=cost(flops, MIB),
        name=name,
    )(pos, *arrays)


def kept(mask, row, col, values):
    return jnp.where(mask[row, col] > 0, values, jnp.zeros_like(values))


def mask_kernel(mask_out, mask_in, w_out, w_in, theirs, out):
    out[1536:1600, 0:768] = theirs[...]
    out[1536:1600, 768:1536] = theirs[...]

    @pl.loop(0, 6)
    def _(i):
        rows = pl.ds(pl.multiple_of(i * 128, 128), 128)
        later = pl.ds(pl.multiple_of(i * 128 + 768, 128), 128)
        for j in range(12):
            cols = slice(j * 128, j * 128 + 128)
            out[rows, cols] = kept(mask_out, i, j, w_out[rows, cols])
            side, tile = j // 6, j % 6
            source = pl.ds(pl.multiple_of(i * 128 + side * 768, 128), 128)
            part = w_in[source, tile * 128 : tile * 128 + 128]
            out[later, cols] = kept(mask_in, i + side * 6, tile, part)


def masked(mask_out, mask_in, w_out, w_in, theirs):
    return pl.pallas_call(
        mask_kernel,
        in_specs=[pl.BlockSpec(memory_space=pltpu.SMEM)] * 2 + in_vmem(3),
        out_specs=pl.BlockSpec(memory_space=pltpu.VMEM),
        out_shape=jax.ShapeDtypeStruct((1600, 1536), BF),
        compiler_params=params(VMEM),
        cost_estimate=cost(0, 4 * MIB),
        name="masked",
    )(mask_out, mask_in, w_out, w_in, theirs)


def values_kernel(pos, pre, hidden, slopes, other):
    core = pos[4]
    zval = pre[...].astype(F32)
    tval = jnp.tanh(coef * (zval + 0.044715 * zval**3))
    hidden[...] = (0.5 * zval * (1.0 + tval)).astype(BF)
    for half in range(2):
        first = lax.rem(pos[3] + half, 2) * 64
        mine = pl.ds(pl.multiple_of(first + core * 32, 32), 32)
        theirs = pl.ds(pl.multiple_of(first + (1 - core) * 32, 32), 32)
        rows = slice(half * 32, half * 32 + 32)
        slopes[rows, :] = slope(pre[mine, :])
        other[rows, :] = pre[theirs, :]


def first_kernel(plan, pos, *refs):
    pieces = refs[: len(plan)]
    own_ref, peer_ref, rows, ins0, ins1 = refs[len(plan) : len(plan) + 5]
    outs, held = refs[len(plan) + 5 : -1], refs[-1]
    for ref, spots in zip(pieces, plan):
        for first, off, half in spots:
            rows[place_z(pos, off, half), :] = ref[first : first + 32, :]

    ins0[...] = rows[512:640, :]
    ins1[...] = rows[640:768, :]

    for half, weight in enumerate((own_ref, peer_ref)):
        held[...] = lax.dot_general(
            rows[0:512, :], weight[0:768, :], NT, preferred_element_type=F32
        )
        where = slice(half * 768, half * 768 + 768)

        for ref, (off, y, _) in zip(outs, TO_X):
            for k, place in enumerate(place_x(pos, off, y)):
                ref[k * 32 : k * 32 + 32, where] = held[place, :].astype(ref.dtype)


def first(pos, pieces, own, peer):
    heights = [(768, BF), (128, BF), (128, BF)] + [(64, kind) for _, _, kind in TO_X]
    return call(
        functools.partial(first_kernel, plan_z()),
        "first",
        pos,
        [*pieces, own, peer],
        [((n, 1536), t) for n, t in heights],
        [pltpu.VMEM((512, 768), F32)],
        4 * 512 * 1536 * 1536,
    )


def second_kernel(pos, *refs):
    pieces, refs = refs[: len(FROM_X)], refs[len(FROM_X) :]
    in_other0, in_other1, own_ref, peer_ref, rows, pack = refs[:6]
    outs = refs[6:-2]
    rows_peer, held = refs[-2:]
    for ref, (off, y) in zip(pieces, FROM_X):
        for k, place in enumerate(place_x(pos, off, y)):
            at = slice(k * 32, k * 32 + 32)
            rows[place, :] = ref[at, 0:768]
            rows_peer[place, :] = ref[at, 768:1536]
    pack[0:128, :] = in_other0[...]
    pack[128:256, :] = in_other1[...]
    pack[256:512, 0:768] = rows_peer[0:256, :]
    pack[256:512, 768:1536] = rows_peer[256:512, :]

    for step in range(2):
        where = slice(step * 768, step * 768 + 768)
        out = lax.dot_general(rows[...], own_ref[768:1536, where], NT, preferred_element_type=F32)
        out += lax.dot_general(
            rows_peer[...], peer_ref[768:1536, where], NT, preferred_element_type=F32
        )
        held[...] = out

        def put(ref, at, off, half):
            ref[at : at + 32, where] = held[place_z(pos, off, half), :].astype(ref.dtype)

        up, down, keep = outs[0:4], outs[4:8], outs[8]
        for s in range(4):
            put(up[s], 0, 4 - s, 0)
            put(down[s], 0, s - 4, 1)
            if s < 3:
                put(up[s], 32, 3 - s, 1)
                put(down[s], 32, s - 3, 0)
        put(keep, 0, 0, 0)
        put(keep, 32, 0, 1)


def second(pos, pieces, in_other, own, peer):
    ring = [(64, BF), (64, F32), (64, F32), (32, F32)]
    shapes = [((512, 768), BF), ((512, 1536), BF)]
    shapes += [((n, 1536), t) for n, t in ring + ring + [(64, F32)]]
    return call(
        second_kernel,
        "second",
        pos,
        [*pieces, *in_other, own, peer],
        shapes,
        [pltpu.VMEM((512, 768), BF), pltpu.VMEM((512, 768), F32)],
        4 * 512 * 1536 * 1536,
    )


def store_kept(total, mask, first, out):
    for i in range(out.shape[0] // 128):
        rows = slice(i * 128, i * 128 + 128)
        for j in range(out.shape[1] // 128):
            cols = slice(j * 128, j * 128 + 128)
            out[rows, cols] = kept(mask, first + i, j, total[rows, cols]).astype(BF)


def wout_kernel(plan, pos, mask, *refs):
    pieces = refs[: len(plan)]
    own, peer, out, held = refs[len(plan) :]
    for ref, spots in zip(pieces, plan):
        for first, off, half in spots:
            owner = lax.rem(pos[0] + half, 2) * 4 + lax.rem(pos[1] + (off + 4), 4)
            held[owner] = ref[first : first + 128, :].reshape(2, 2, 32, -1)
    total = None
    for k, part in enumerate((own, peer)):
        core = lax.rem(pos[4] + k, 2)
        halves = [held[:, lax.rem(pos[3] + y, 2), core].reshape(256, -1) for y in range(2)]
        left = jnp.concatenate(halves)
        term = lax.dot_general(left, part[0:512, :], TN, preferred_element_type=F32)
        total = term if total is None else total + term
    store_kept(total, mask, pl.program_id(0) * (out.shape[0] // 128), out)


def wout_grad(pos, pieces, own, peer, mask):
    block = 384
    return pl.pallas_call(
        functools.partial(wout_kernel, plan_x(128)),
        grid_spec=pltpu.PrefetchScalarGridSpec(
            num_scalar_prefetch=2,
            grid=(768 // block,),
            in_specs=[pl.BlockSpec((a.shape[0], block), lambda i, *_: (0, i)) for a in pieces]
            + in_vmem(2),
            out_specs=pl.BlockSpec((block, 1536), lambda i, *_: (i, 0)),
            scratch_shapes=[pltpu.VMEM((8, 2, 2, 32, block), BF)],
        ),
        out_shape=jax.ShapeDtypeStruct((768, 1536), BF),
        compiler_params=params(VMEM),
        cost_estimate=cost(4 * 1024 * 1536 * 768, 8 * MIB),
        name="wout_grad",
    )(pos, mask, *pieces, own, peer)


def win_kernel(mask, in0, in1, peer0, peer1, acts, peer, out):
    left = jnp.concatenate([in0[...], in1[...]])
    total = lax.dot_general(left, acts[...], TN, preferred_element_type=F32)
    left = jnp.concatenate([peer0[...], peer1[...]])
    right = jnp.concatenate([peer[256:512, 0:768], peer[256:512, 768:1536]])
    total += lax.dot_general(left, right, TN, preferred_element_type=F32)
    store_kept(total, mask, pl.program_id(0) * (out.shape[0] // 128), out)


def win_grad(rows, pack, rows_peer, pack_peer, acts, mask):
    block = 768
    at = lambda k: pl.BlockSpec((256, block), lambda i, _: (k, i))
    return pl.pallas_call(
        win_kernel,
        grid_spec=pltpu.PrefetchScalarGridSpec(
            num_scalar_prefetch=1,
            grid=(1536 // block,),
            in_specs=[at(2), at(0), at(2), at(0)] + in_vmem(2),
            out_specs=pl.BlockSpec((block, 768), lambda i, _: (i, 0)),
        ),
        out_shape=jax.ShapeDtypeStruct((1536, 768), BF),
        compiler_params=params(VMEM),
        cost_estimate=cost(4 * 1024 * 1536 * 768, 8 * MIB),
        name="win_grad",
    )(mask, rows, pack, rows_peer, pack_peer, acts, pack_peer)


def slope(values):
    zval = values.astype(F32)
    tval = jnp.tanh(coef * (zval + 0.044715 * zval**3))
    return 0.5 * (1.0 + tval) + 0.5 * zval * (1.0 - tval * tval) * coef * (
        1.0 + 3.0 * 0.044715 * zval * zval
    )


def body(inputs, grad_out, pre_act, w_in, w_out, mask_in, mask_out):
    names = ("yhi", "x", "z", "ylo", "core")
    pos = jnp.stack([lax.axis_index(n) for n in names]).astype(jnp.int32)
    f = lambda v: v.astype(F32)
    count, two = 32, 64

    other = shift(grad_out, "ylo", 1)
    shapes = [((128, 768), BF), ((64, 768), F32), ((64, 768), BF)]
    hidden, slopes, theirs = call(values_kernel, "values", pos, [pre_act], shapes, [], MIB)
    hidden_other = shift(hidden, "yhi", 1)
    other, hidden, theirs = together(other, hidden, theirs)
    sent = jnp.concatenate([grad_out, other, inputs])
    up1, down1 = both_ways("z", sent, sent)
    own = masked(after(mask_out, sent), mask_in, w_out, w_in, theirs)
    up1, down1, own, hidden_other = together(up1, down1, own, hidden_other)
    up2, down2 = both_ways("z", up1, down1)
    peer = shift(own, "core", 1)
    hid = jnp.concatenate([hidden, hidden_other])
    hid_up, hid_down = both_ways("x", hid, hid)
    up2, down2 = together(up2, down2)
    up3, down3 = both_ways("z", up2, down2)
    up3, down3, hid_up, hid_down = together(up3, down3, hid_up, hid_down)
    up4, down4 = both_ways("z", up3[:64], down3[64:])
    hid_far = shift(after(hid_up, up3), "x", 1)
    up4, down4, hid_far = together(up4, down4, hid_far)
    pieces = [sent, up1, down1, up2, down2, up3, down3, up4, down4]

    rows, ins0, ins1, far1, down1, up1, far0, up0, down0, keep0, keep1 = first(pos, pieces, own, peer)
    got, down1 = both_ways("x", far1, down1)
    in_other = shift(ins0, "ylo", 1)
    slopes = jnp.concatenate([slopes, slope(after(peer, keep1)[1536:, :768])], axis=1)
    rows_peer = shift(after(rows, slopes), "core", 1)
    got, down1, slopes = together(got, down1, slopes)
    up1, got = both_ways("x", (up1 + f(got)).astype(BF), far0)
    up1, got, in_other = together(up1, got, in_other)
    other = shift((keep1 + f(down1) + f(up1)).astype(BF), "yhi", 1)
    up0, down0 = both_ways("x", up0, (down0 + f(got)).astype(BF))
    act = ((keep0 + f(up0) + f(down0) + f(other)) * slopes).astype(BF)

    other = shift(act, "yhi", 1)
    up0, down0 = both_ways("x", act, act)
    hidden_pieces = [hid, hid_up, hid_down, hid_far]
    grad_w_out = wout_grad(pos, hidden_pieces, rows, after(rows_peer, act), mask_out)
    other, up0, down0, grad_w_out = together(other, up0, down0, grad_w_out)
    up1, down1 = both_ways("x", other, other)
    in_other = [in_other, shift(after(ins1, other), "ylo", 1)]
    far0 = shift(up0, "x", 1)
    far1 = shift(down1, "x", -1)

    acts = [act, other, up0, down0, up1, down1, far0, far1]
    outs = second(pos, acts, in_other, own, peer)
    acts, pack = outs[0:2]
    up, down, keep = outs[2:6], outs[6:10], outs[10]
    send_up, send_down = up[0], down[0]
    for s in range(1, 4):
        got_up, got_down = shift(send_up, "z", 1), shift(send_down, "z", -1)
        if s == 1:
            pack_peer = shift(pack, "core", 1)
        elif s == 3:
            grad_w_in = win_grad(
                rows, pack, rows_peer, after(pack_peer, send_up, send_down), acts, mask_in
            )
            got_up, got_down, _ = lax.optimization_barrier((got_up, got_down, grad_w_in))
        n = two if s < 3 else count
        send_up = (up[s] + f(got_up[:n])).astype(BF)
        send_down = (down[s] + f(got_down[:n])).astype(BF)
    end_up, end_down = shift(send_up, "z", 1), shift(send_down, "z", -1)
    send = (keep[count:] + f(got_up[count:]) + f(end_down)).astype(BF)
    mine = keep[:count] + f(got_down[count:]) + f(end_up)
    grad_inputs = (mine + f(shift(send, "ylo", 1))).astype(BF)
    return grad_inputs, grad_w_in, grad_w_out


def solution(mesh):
    fine = Mesh(mesh.devices.reshape(2, 4, 8, 2, 2), ("yhi", "x", "z", "ylo", "core"))
    row, col = ("yhi", "x"), ("z", "ylo", "core")
    return jax.shard_map(
        body,
        mesh=fine,
        in_specs=(
            P(col, row),
            P(col, row),
            P(row, col),
            P(row, col),
            P(col, row),
            P(row, col),
            P(col, row),
        ),
        out_specs=(P(col, row), P(row, col), P(col, row)),
        check_vma=False,
    )
```
